32 devices in a mesh: gx: 8 (over y, x, core), gy: 4 (over z).
Axes of the slice: x: 2, y: 2, z: 4, core: 2. Of those that a mesh axis runs over, the one named last changes fastest.
Arguments:
- multipoles: float32 [10, 262144], P(None, ('gx', 'gy')), may hold values from -8 to 8
- fractions: float32 [3, 262144], P(None, ('gx', 'gy')), may hold values from 0 to 1
- base_index: int32 [3, 262144], P(None, ('gx', 'gy')), may hold values from 0 to 252, as said below
- block_plane: int32 [2048], P(('gx', 'gy')), may hold values from 0 to 7
- atom_count: int32 [2048], P(('gx', 'gy')), may hold values from 32 to 128, as said below
- coupling: float32 [8, 256, 256], replicated, may hold values from -0.375 to 0.375
Outputs:
- coupled: float32 [2, 256, 512, 256], P(None, ('gx', 'gy'))
The draws below stay inside these ranges and needn't reach their ends.
Inputs may be any that keep to these rules, and one draw needn't show every extreme that they name: `base_index`: row 0 is an atom's x cell within its block's plane block, 0 to 7; row 1 its y cell within its device's 128 columns, 0 to 127; row 2 its z cell, 0 to 252. Atoms of the slots of device d lie in device d's cells. `atom_count`: slots of a block at or past its count are padding whose values are to be ignored.
All inputs are finite; a program needn't handle non-finite values.
Results may differ from the reference program's by a relative error of at most 0.0042.
Values sent between devices are 32-bit elements; how exact they have to be, the bound alone decides.
A program may use at most 128 MiB of HBM per device.

```python
import math
import jax
import jax.numpy as jnp
from jax import lax

NX = 512
NY = 512
NZ = 256
XB = 8
SLOT_BLK = 128
MBLK = 8
KX = 256
CX = 64
CY = 128
SLOTS_DEV = 8192
BLOCKS = 2048
SLOTS = 262144
N_GY = 4


def draw_base_index(key, part):
    keys = jax.random.split(jax.random.fold_in(key, 3), 3)
    x_part = jax.random.randint(keys[0], (SLOTS,), 0, XB)
    y_part = jax.random.randint(keys[1], (SLOTS,), 0, CY)
    z_part = jax.random.randint(keys[2], (SLOTS,), 0, NZ - 3)
    slot_ids = jnp.arange(SLOTS, dtype=jnp.int32)
    x_part = jnp.where(slot_ids == 0, XB - 1, jnp.where(slot_ids == 1, 0, x_part))
    y_part = jnp.where(slot_ids == 0, CY - 1, jnp.where(slot_ids == 1, 0, y_part))
    z_part = jnp.where(slot_ids == 0, NZ - 4, jnp.where(slot_ids == 1, 0, z_part))
    return jnp.stack([x_part, y_part, z_part]).astype(jnp.int32)


def draw_atom_count(key, part):
    counts = jax.random.randint(jax.random.fold_in(key, 5), (BLOCKS,), 32, 129)
    chosen = jax.random.randint(jax.random.fold_in(key, 6), (), 0, BLOCKS)
    block_ids = jnp.arange(BLOCKS, dtype=jnp.int32)
    return jnp.where(block_ids == chosen, 128, counts).astype(jnp.int32)


def with_ends(values, key, smallest, largest):
    longest = values.shape.index(max(values.shape))
    spots = []
    for shift in (0, 1):
        where = [jax.random.randint(jax.random.fold_in(key, axis), (), 0, length) for axis, length in enumerate(values.shape)]
        where[longest] = (where[longest] + shift) % values.shape[longest]
        spots.append(tuple(where))
    return values.at[spots[0]].set(smallest).at[spots[1]].set(largest)


def levels(rng, extent, pieces, low, high):
    def one(dim, blocks):
        draws = jax.random.uniform(jax.random.fold_in(jax.random.fold_in(rng, 6), dim), (blocks,), jnp.float32, low / len(pieces), high / len(pieces))
        return jnp.repeat(jnp.exp(draws), extent[dim] // blocks).reshape((-1,) + (1,) * (len(extent) - dim - 1))

    gain = one(*pieces[0])
    for cut in pieces[1:]:
        gain = gain * one(*cut)
    return gain


def normal_values(own_key, extent, spread, limit, cuts=(), kind=jnp.bfloat16):
    values = spread * jax.random.normal(own_key, extent, jnp.float32)
    if cuts:
        values = values * levels(own_key, extent, cuts, -0.22, 0.18)
    return jnp.clip(values, -limit, limit).astype(kind)


def setup_inputs(seed: int = 0) -> dict:
    splits = jax.random.split(jax.random.key(seed), 7)
    multipoles = normal_values(splits[0], (10, SLOTS), 2.0, 8.0, ((1, 32),), jnp.float32)
    fractions = jnp.clip(1.0 * jax.random.uniform(splits[1], (3, SLOTS), jnp.float32) ** levels(splits[1], (3, SLOTS), ((1, 32),), -0.2, 0.2), 0.0, 1.0)
    base_index = draw_base_index(jax.random.fold_in(splits[6], 71), 0)
    block_plane = with_ends(jax.random.randint(splits[3], (BLOCKS,), 0, CX // XB), jax.random.fold_in(splits[3], 1), 0, (CX // XB) - 1).astype(jnp.int32)
    atom_count = draw_atom_count(jax.random.fold_in(splits[6], 71), 0)
    coupling = normal_values(splits[5], (MBLK, NZ, NZ), NZ ** -0.5, 0.375, (), jnp.float32)
    return dict(multipoles=multipoles, fractions=fractions, base_index=base_index, block_plane=block_plane, atom_count=atom_count, coupling=coupling)


def spline_weights(fraction):
    remain = 1.0 - fraction
    square = fraction * fraction
    cubed = square * fraction
    values = jnp.stack([remain * remain * remain / 6.0, (3.0 * cubed - 6.0 * square + 4.0) / 6.0, (-3.0 * cubed + 3.0 * square + 3.0 * fraction + 1.0) / 6.0, cubed / 6.0])
    slopes = jnp.stack([-remain * remain / 2.0, (3.0 * square - 4.0 * fraction) / 2.0, (-3.0 * square + 2.0 * fraction + 1.0) / 2.0, square / 2.0])
    curves = jnp.stack([remain, 3.0 * fraction - 2.0, 1.0 - 3.0 * fraction, fraction])
    return jnp.stack([values, slopes, curves])

def plane_weights(moments, spline_x, spline_y):
    x_spline = spline_x[:, :, None]
    y_spline = spline_y[:, None, :]
    moment = moments[:, None, None]
    order_zero = moment[0] * x_spline[0] * y_spline[0] + moment[1] * x_spline[1] * y_spline[0] + moment[2] * x_spline[0] * y_spline[1] + moment[4] * x_spline[2] * y_spline[0] + moment[5] * x_spline[0] * y_spline[2] + moment[7] * x_spline[1] * y_spline[1]
    order_one = moment[3] * x_spline[0] * y_spline[0] + moment[8] * x_spline[1] * y_spline[0] + moment[9] * x_spline[0] * y_spline[1]
    order_two = moment[6] * x_spline[0] * y_spline[0]
    return jnp.stack([order_zero, order_one, order_two]).astype(jnp.bfloat16)

def reference(multipoles, fractions, base_index, block_plane, atom_count, coupling):
    slot_ids = jnp.arange(SLOTS, dtype=jnp.int32)
    block_ids = slot_ids // SLOT_BLK
    live_slot = (slot_ids % SLOT_BLK < atom_count[block_ids]).astype(jnp.float32)
    moments = multipoles * live_slot[None, :]
    device = slot_ids // SLOTS_DEV
    x_cell = device // N_GY * CX + block_plane[block_ids] * XB + base_index[0]
    y_cell = device % N_GY * CY + base_index[1]
    z_cell = base_index[2]
    planes = plane_weights(moments, spline_weights(fractions[0]), spline_weights(fractions[1]))
    planes = lax.optimization_barrier(planes).astype(jnp.float32)
    z_weights = lax.optimization_barrier(spline_weights(fractions[2]).astype(jnp.bfloat16)).astype(jnp.float32)
    contrib = jnp.einsum('kabs,kcs->abcs', planes, z_weights, precision=lax.Precision.HIGHEST)
    tap_ids = jnp.arange(4, dtype=jnp.int32)
    x_full = (x_cell[None, :] + tap_ids[:, None]) % NX
    y_full = (y_cell[None, :] + tap_ids[:, None]) % NY
    z_full = z_cell[None, :] + tap_ids[:, None]
    flat_index = (x_full[:, None, None, :] * NY + y_full[None, :, None, :]) * NZ + z_full[None, None, :, :]
    density = jnp.zeros((NX * NY * NZ,), jnp.float32).at[flat_index.reshape(-1)].add(contrib.reshape(-1))
    density = density.reshape(NX, NY, NZ)
    along_x = jnp.fft.fft(density, axis=0)[:KX]
    spectrum = jnp.fft.fft(along_x, axis=1) / math.sqrt(NX * NY)
    spectra = jnp.stack([jnp.real(spectrum), jnp.imag(spectrum)])
    blocked = spectra.reshape(2, KX, MBLK, NY // MBLK, NZ)
    coupled = jnp.einsum('ckbjw,bzw->ckbjz', blocked, coupling, precision=lax.Precision.HIGHEST)
    return coupled.reshape(2, KX, NY, NZ)
```

```python
import functools
import math

import jax
import jax.numpy as jnp
import numpy as np
from jax import lax
from jax.experimental import pallas as pl
from jax.experimental.pallas import tpu as pltpu
from jax.sharding import PartitionSpec as P

NX = 512
NY = 512
NZ = 256
XB = 8
SLOT_BLK = 128
MBLK = 8
KX = 256
GROUP = 8
PACK = 16


def from_behind(value, axis, by):
    devices = lax.axis_size(axis)
    return lax.ppermute(value, axis, [(i, (i + by) % devices) for i in range(devices)])


def spline_weights(u):
    r = 1.0 - u
    square = u * u
    cubed = square * u
    values = [
        r * r * r / 6.0,
        (3.0 * cubed - 6.0 * square + 4.0) / 6.0,
        (-3.0 * cubed + 3.0 * square + 3.0 * u + 1.0) / 6.0,
        cubed / 6.0,
    ]
    slopes = [
        -r * r / 2.0,
        (3.0 * square - 4.0 * u) / 2.0,
        (-3.0 * square + 2.0 * u + 1.0) / 2.0,
        square / 2.0,
    ]
    curves = [r, 3.0 * u - 2.0, 1.0 - 3.0 * u, u]
    return values, slopes, curves


def spread_kernel(
    plane_ref, count_ref, moment_ref, fraction_ref, cell_ref, out_ref, weight_ref, rows_ref
):
    step = pl.program_id(0)
    rows = out_ref.shape[1]
    padded = rows_ref.shape[1]
    bf16 = jnp.bfloat16

    @pl.when(step == 0)
    def _():
        def clear(plane, carry):
            out_ref[plane] = jnp.zeros((rows, NZ), jnp.float32)
            return carry

        lax.fori_loop(0, out_ref.shape[0], clear, 0)

    wx, dx, sx = spline_weights(fraction_ref[0])
    wy, dy, sy = spline_weights(fraction_ref[1])
    z_taps = spline_weights(fraction_ref[2])
    m = [moment_ref[i] for i in range(10)]
    for a in range(4):
        base = m[0] * wx[a] + m[1] * dx[a] + m[4] * sx[a]
        slope = m[2] * wx[a] + m[7] * dx[a]
        curve = m[5] * wx[a]
        one_base = m[3] * wx[a] + m[8] * dx[a]
        one_slope = m[9] * wx[a]
        two = m[6] * wx[a]
        for b in range(4):
            weight_ref[a * 4 + b] = base * wy[b] + slope * dy[b] + curve * sy[b]
            weight_ref[16 + a * 4 + b] = one_base * wy[b] + one_slope * dy[b]
            weight_ref[32 + a * 4 + b] = two * wy[b]
    for k in range(3):
        for c in range(4):
            weight_ref[48 + k * 4 + c] = z_taps[k][c]

    lane = lax.broadcasted_iota(jnp.int32, (1, SLOT_BLK), 1)

    def spans(tile, count):
        return jnp.concatenate([tile] * count, axis=0)

    def packed(row):
        return jnp.broadcast_to(row, (PACK, SLOT_BLK)).astype(bf16)

    y_count = padded // PACK
    z_count = NZ // PACK

    def one_block(g, carry):
        block = step * GROUP + g
        alive = lane < count_ref[block]
        x_cell = packed(cell_ref[0, pl.ds(g, 1), :].astype(jnp.float32))
        y_row = jnp.where(alive, cell_ref[1, pl.ds(g, 1), :], -1024).astype(jnp.float32)
        z_row = cell_ref[2, pl.ds(g, 1), :].astype(jnp.float32)

        def weight(index):
            return packed(weight_ref[index, pl.ds(g, 1), :])

        def chosen(hits, index, count):
            zero = jnp.zeros((count * PACK, SLOT_BLK), bf16)
            total = zero
            for tap in range(4):
                total = jnp.where(hits[tap], spans(weight(index + tap), count), total)
            return total

        y_ids = lax.broadcasted_iota(jnp.int32, (padded, SLOT_BLK), 0).astype(jnp.float32)
        y_ids = y_ids.astype(bf16)
        y_hits = [y_ids == spans(packed(y_row + float(b)), y_count) for b in range(4)]
        for k in range(3):
            for a in range(4):
                rows_ref[k * 4 + a] = chosen(y_hits, k * 16 + a * 4, y_count)
        z_ids = lax.broadcasted_iota(jnp.int32, (NZ, SLOT_BLK), 0).astype(jnp.float32)
        z_ids = z_ids.astype(bf16)
        z_hits = [z_ids == spans(packed(z_row + float(c)), z_count) for c in range(4)]
        z_window = jnp.concatenate(
            [chosen(z_hits, 48 + k * 4, z_count) for k in range(3)], axis=1
        )
        plane = plane_ref[block] * XB
        zero = jnp.zeros((padded, SLOT_BLK), bf16)
        for first, count in ((0, 4), (4, 4), (8, 3)):
            parts = []
            for x in range(first, first + count):
                pieces = []
                for k in range(3):
                    total = zero
                    for a in range(4):
                        if 0 <= x - a < XB:
                            hit = x_cell == jnp.full((PACK, SLOT_BLK), x - a, bf16)
                            total = jnp.where(spans(hit, y_count), rows_ref[k * 4 + a], total)
                    pieces.append(total)
                parts.append(jnp.concatenate(pieces, axis=1))
            window = jnp.concatenate(parts, axis=0)
            result = lax.dot_general(
                window, z_window, (((1,), (1,)), ((), ())), preferred_element_type=jnp.float32
            )
            for i in range(count):
                out_ref[plane + first + i] += result[i * padded : i * padded + rows]
        return carry

    lax.fori_loop(0, GROUP, one_block, 0)


def spread(multipoles, fractions, base_index, block_plane, atom_count, cells_x, cells_y):
    blocks = block_plane.shape[0]
    rows = -(-(cells_y + 3) // 8) * 8
    padded = -(-(cells_y + 3) // PACK) * PACK

    def part(height):
        return pl.BlockSpec((height, GROUP, SLOT_BLK), lambda i, *_: (0, i, 0))

    return pl.pallas_call(
        spread_kernel,
        out_shape=jax.ShapeDtypeStruct((cells_x + 3, rows, NZ), jnp.float32),
        grid_spec=pltpu.PrefetchScalarGridSpec(
            num_scalar_prefetch=2,
            grid=(blocks // GROUP,),
            in_specs=[part(10), part(3), part(3)],
            out_specs=pl.BlockSpec((cells_x + 3, rows, NZ), lambda i, *_: (0, 0, 0)),
            scratch_shapes=[
                pltpu.VMEM((60, GROUP, SLOT_BLK), jnp.float32),
                pltpu.VMEM((12, padded, SLOT_BLK), jnp.bfloat16),
            ],
        ),
        compiler_params=pltpu.CompilerParams(vmem_limit_bytes=48 * 1024 * 1024),
    )(
        block_plane,
        atom_count,
        multipoles.reshape(10, blocks, SLOT_BLK),
        fractions.reshape(3, blocks, SLOT_BLK),
        base_index.reshape(3, blocks, SLOT_BLK),
    )


def phases(waves, cells, size):
    return (np.arange(waves)[:, None] * np.arange(cells)[None, :] % size) * (2.0 * math.pi / size)


def per_device(multipoles, fractions, base_index, block_plane, atom_count, coupling):
    cells_x = NX // lax.axis_size("gx")
    cells_y = NY // lax.axis_size("gy")
    extended = spread(
        multipoles, fractions, base_index, block_plane, atom_count, cells_x, cells_y
    )
    rim_x = from_behind(extended[cells_x:, : cells_y + 3], "gx", 1)
    spill = extended[:cells_x, cells_y : cells_y + 3].at[:3].add(rim_x[:, cells_y:])
    rim_y = from_behind(spill, "gy", 1)
    density = (
        extended[:cells_x, :cells_y]
        + jnp.pad(rim_x[:, :cells_y], ((0, cells_x - 3), (0, 0), (0, 0)))
        + jnp.pad(rim_y, ((0, 0), (0, cells_y - 3), (0, 0)))
    )
    phase_x = phases(KX, NX, NX)
    scale = 1.0 / math.sqrt(NX * NY)
    table_x = np.concatenate([np.cos(phase_x) * scale, -np.sin(phase_x) * scale], 0)
    lines = lax.all_to_all(density, "gx", split_axis=1, concat_axis=0, tiled=True)
    result = jnp.einsum("kx,xyz->kyz", jnp.asarray(table_x, jnp.float32), lines, precision=lax.Precision.HIGH)
    spectrum = result.reshape(2, KX, lines.shape[1], lines.shape[2])
    spectrum = lax.all_to_all(
        lax.all_to_all(spectrum, "gx", split_axis=1, concat_axis=2, tiled=True),
        "gy",
        split_axis=1,
        concat_axis=2,
        tiled=True,
    )
    phase_y = phases(NY, NY, NY)
    cosine, sine = np.cos(phase_y), np.sin(phase_y)
    table_y = jnp.asarray(np.stack([np.stack([cosine, sine]), np.stack([-sine, cosine])]), jnp.float32)
    waves = jnp.einsum("cdqr,dkrz->ckqz", table_y, spectrum, precision=lax.Precision.HIGH)
    mode_rows = waves.shape[1]
    stacked = waves.reshape(2, mode_rows, MBLK, NY // MBLK, NZ)
    coupled = jnp.einsum("ckbjw,bzw->ckbjz", stacked, coupling)
    return coupled.reshape(2, mode_rows, NY, NZ)


def solution(mesh):
    return jax.shard_map(
        per_device,
        mesh=mesh,
        in_specs=(
            P(None, ("gx", "gy")),
            P(None, ("gx", "gy")),
            P(None, ("gx", "gy")),
            P(("gx", "gy")),
            P(("gx", "gy")),
            P(),
        ),
        out_specs=P(None, ("gx", "gy"), None, None),
        check_vma=False,
    )
```

```python
import functools
import math

import jax
import jax.numpy as jnp
import numpy as np
from jax import lax
from jax.experimental import pallas as pl
from jax.experimental.pallas import tpu as pltpu
from jax.sharding import PartitionSpec as P

NX = 512
NY = 512
NZ = 256
XB = 8
SLOT_BLK = 128
MBLK = 8
KX = 256
GROUP = 8
PACK = 16


def from_behind(value, axis, by):
    devices = lax.axis_size(axis)
    return lax.ppermute(value, axis, [(i, (i + by) % devices) for i in range(devices)])


def spline_weights(u):
    r = 1.0 - u
    square = u * u
    cubed = square * u
    values = [
        r * r * r / 6.0,
        (3.0 * cubed - 6.0 * square + 4.0) / 6.0,
        (-3.0 * cubed + 3.0 * square + 3.0 * u + 1.0) / 6.0,
        cubed / 6.0,
    ]
    slopes = [
        -r * r / 2.0,
        (3.0 * square - 4.0 * u) / 2.0,
        (-3.0 * square + 2.0 * u + 1.0) / 2.0,
        square / 2.0,
    ]
    curves = [r, 3.0 * u - 2.0, 1.0 - 3.0 * u, u]
    return values, slopes, curves


def spread_kernel(
    plane_ref, count_ref, moment_ref, fraction_ref, cell_ref, out_ref, weight_ref, rows_ref
):
    step = pl.program_id(0)
    rows = out_ref.shape[1]
    padded = rows_ref.shape[1]
    bf16 = jnp.bfloat16

    @pl.when(step == 0)
    def _():
        def clear(plane, carry):
            out_ref[plane] = jnp.zeros((rows, NZ), jnp.float32)
            return carry

        lax.fori_loop(0, out_ref.shape[0], clear, 0)

    wx, dx, sx = spline_weights(fraction_ref[0])
    wy, dy, sy = spline_weights(fraction_ref[1])
    z_taps = spline_weights(fraction_ref[2])
    m = [moment_ref[i] for i in range(10)]
    for a in range(4):
        base = m[0] * wx[a] + m[1] * dx[a] + m[4] * sx[a]
        slope = m[2] * wx[a] + m[7] * dx[a]
        curve = m[5] * wx[a]
        one_base = m[3] * wx[a] + m[8] * dx[a]
        one_slope = m[9] * wx[a]
        two = m[6] * wx[a]
        for b in range(4):
            weight_ref[a * 4 + b] = base * wy[b] + slope * dy[b] + curve * sy[b]
            weight_ref[16 + a * 4 + b] = one_base * wy[b] + one_slope * dy[b]
            weight_ref[32 + a * 4 + b] = two * wy[b]
    for k in range(3):
        for c in range(4):
            weight_ref[48 + k * 4 + c] = z_taps[k][c]

    lane = lax.broadcasted_iota(jnp.int32, (1, SLOT_BLK), 1)

    def spans(tile, count):
        return jnp.concatenate([tile] * count, axis=0)

    def packed(row):
        return jnp.broadcast_to(row, (PACK, SLOT_BLK)).astype(bf16)

    y_count = padded // PACK
    z_count = NZ // PACK

    def one_block(g, carry):
        block = step * GROUP + g
        alive = lane < count_ref[block]
        x_cell = packed(cell_ref[0, pl.ds(g, 1), :].astype(jnp.float32))
        y_row = jnp.where(alive, cell_ref[1, pl.ds(g, 1), :], -1024).astype(jnp.float32)
        z_row = cell_ref[2, pl.ds(g, 1), :].astype(jnp.float32)

        def weight(index):
            return packed(weight_ref[index, pl.ds(g, 1), :])

        def chosen(hits, index, count):
            zero = jnp.zeros((count * PACK, SLOT_BLK), bf16)
            total = zero
            for tap in range(4):
                total = jnp.where(hits[tap], spans(weight(index + tap), count), total)
            return total

        y_ids = lax.broadcasted_iota(jnp.int32, (padded, SLOT_BLK), 0).astype(jnp.float32)
        y_ids = y_ids.astype(bf16)
        y_hits = [y_ids == spans(packed(y_row + float(b)), y_count) for b in range(4)]
        for k in range(3):
            for a in range(4):
                rows_ref[k * 4 + a] = chosen(y_hits, k * 16 + a * 4, y_count)
        z_ids = lax.broadcasted_iota(jnp.int32, (NZ, SLOT_BLK), 0).astype(jnp.float32)
        z_ids = z_ids.astype(bf16)
        z_hits = [z_ids == spans(packed(z_row + float(c)), z_count) for c in range(4)]
        z_window = jnp.concatenate(
            [chosen(z_hits, 48 + k * 4, z_count) for k in range(3)], axis=1
        )
        plane = plane_ref[block] * XB
        zero = jnp.zeros((padded, SLOT_BLK), bf16)
        for first, count in ((0, 4), (4, 4), (8, 3)):
            parts = []
            for x in range(first, first + count):
                pieces = []
                for k in range(3):
                    total = zero
                    for a in range(4):
                        if 0 <= x - a < XB:
                            hit = x_cell == jnp.full((PACK, SLOT_BLK), x - a, bf16)
                            total = jnp.where(spans(hit, y_count), rows_ref[k * 4 + a], total)
                    pieces.append(total)
                parts.append(jnp.concatenate(pieces, axis=1))
            window = jnp.concatenate(parts, axis=0)
            result = lax.dot_general(
                window, z_window, (((1,), (1,)), ((), ())), preferred_element_type=jnp.float32
            )
            for i in range(count):
                out_ref[plane + first + i] += result[i * padded : i * padded + rows]
        return carry

    lax.fori_loop(0, GROUP, one_block, 0)


def spread(multipoles, fractions, base_index, block_plane, atom_count, cells_x, cells_y):
    blocks = block_plane.shape[0]
    rows = -(-(cells_y + 3) // 8) * 8
    padded = -(-(cells_y + 3) // PACK) * PACK

    def part(height):
        return pl.BlockSpec((height, GROUP, SLOT_BLK), lambda i, *_: (0, i, 0))

    return pl.pallas_call(
        spread_kernel,
        out_shape=jax.ShapeDtypeStruct((cells_x + 3, rows, NZ), jnp.float32),
        grid_spec=pltpu.PrefetchScalarGridSpec(
            num_scalar_prefetch=2,
            grid=(blocks // GROUP,),
            in_specs=[part(10), part(3), part(3)],
            out_specs=pl.BlockSpec((cells_x + 3, rows, NZ), lambda i, *_: (0, 0, 0)),
            scratch_shapes=[
                pltpu.VMEM((60, GROUP, SLOT_BLK), jnp.float32),
                pltpu.VMEM((12, padded, SLOT_BLK), jnp.bfloat16),
            ],
        ),
        compiler_params=pltpu.CompilerParams(vmem_limit_bytes=48 * 1024 * 1024),
    )(
        block_plane,
        atom_count,
        multipoles.reshape(10, blocks, SLOT_BLK),
        fractions.reshape(3, blocks, SLOT_BLK),
        base_index.reshape(3, blocks, SLOT_BLK),
    )


def phases(waves, cells, size):
    return (np.arange(waves)[:, None] * np.arange(cells)[None, :] % size) * (2.0 * math.pi / size)


def exchange_kernel(
    n_gx,
    n_gy,
    chunks_y,
    grid_ref,
    high_ref,
    low_ref,
    out_ref,
    lines_ref,
    waves_ref,
    send_x,
    recv_x,
    send_k,
    recv_k,
    own_x,
    own_k,
):
    gx = lax.axis_index("gx")
    gy = lax.axis_index("gy")
    devices = n_gx * n_gy
    tall, cells_x = lines_ref.shape[0], grid_ref.shape[1]
    height = tall // chunks_y
    padded = waves_ref.shape[2]
    tile = padded // chunks_y
    modes = KX // devices
    chunks = [(i, j) for j in range(2) for i in range(chunks_y)]
    f32, bf16 = jnp.float32, jnp.bfloat16

    def coords(r):
        return lax.rem(gx + r // n_gy, n_gx), lax.rem(gy + lax.rem(r, n_gy), n_gy)

    barrier = pltpu.get_barrier_semaphore()

    def greet(r, carry):
        tx, ty = coords(r)
        pl.semaphore_signal(
            barrier, inc=1, device_id=(tx, ty), device_id_type=pl.DeviceIdType.MESH
        )
        return carry

    lax.fori_loop(1, devices, greet, 0)
    pl.semaphore_wait(barrier, devices - 1)

    def line_refs(n, tx):
        i, j = chunks[n]
        lanes = pl.ds(j * 128, 128)
        source = grid_ref.at[pl.ds(tx * tall + i * height, height), :, lanes]
        target = lines_ref.at[
            pl.ds(i * height, height), pl.ds(pl.multiple_of(gx * cells_x, cells_x), cells_x), lanes
        ]
        return source, target

    def line_copy(n, r):
        tx = lax.rem(gx + r, n_gx)
        source, target = line_refs(n, tx)
        return pltpu.make_async_remote_copy(
            src_ref=source,
            dst_ref=target,
            send_sem=send_x.at[n, r],
            recv_sem=recv_x.at[n, r],
            device_id=(tx, gy),
            device_id_type=pl.DeviceIdType.MESH,
        )

    def wave_refs(n, rank):
        i, j = chunks[n]
        lanes = pl.ds(j * 128, 128)
        span = pl.ds(i * tile, tile)
        source = waves_ref.at[:, pl.ds(rank * modes, modes), span, lanes]
        target = out_ref.at[:, :, gy * n_gx + gx, span, lanes]
        return source, target

    def wave_copy(n, r):
        tx, ty = coords(r)
        source, target = wave_refs(n, tx * n_gy + ty)
        return pltpu.make_async_remote_copy(
            src_ref=source,
            dst_ref=target,
            send_sem=send_k.at[n, r],
            recv_sem=recv_k.at[n, r],
            device_id=(tx, ty),
            device_id_type=pl.DeviceIdType.MESH,
        )

    def own_line(n):
        source, target = line_refs(n, gx)
        return pltpu.make_async_copy(source, target, own_x.at[n])

    def own_wave(n):
        source, target = wave_refs(n, gx * n_gy + gy)
        return pltpu.make_async_copy(source, target, own_k.at[n])

    def each(first, last, act):
        def body(r, carry):
            act(r)
            return carry

        lax.fori_loop(first, last, body, 0)

    for n in range(len(chunks)):
        each(1, n_gx, lambda r: line_copy(n, r).start())
        own_line(n).start()
    for n, (i, j) in enumerate(chunks):
        each(1, n_gx, lambda r: line_copy(n, r).wait_recv())
        own_line(n).wait()
        lanes = pl.ds(j * 128, 128)
        for first in range(i * height, (i + 1) * height, 2):
            picked = [y for y in (first, first + 1) if y < (i + 1) * height]
            block = jnp.concatenate([lines_ref[y, :, lanes] for y in picked], axis=1)
            top = block.astype(bf16)
            rest = (block - top.astype(f32)).astype(bf16)
            high = high_ref[...]
            value = jnp.dot(high, top, preferred_element_type=f32)
            value += jnp.dot(high, rest, preferred_element_type=f32)
            value += jnp.dot(low_ref[...], top, preferred_element_type=f32)
            for index, y in enumerate(picked):
                row = y if tall % 8 == 0 else y - i * height
                part = value[:, index * 128 : (index + 1) * 128]
                waves_ref[0, :, row, lanes] = part[:KX]
                waves_ref[1, :, row, lanes] = part[KX:]
        each(1, devices, lambda r: wave_copy(n, r).start())
        own_wave(n).start()
    for n in range(len(chunks)):
        each(1, n_gx, lambda r: line_copy(n, r).wait_send())
        each(1, devices, lambda r: wave_copy(n, r).wait_recv())
        each(1, devices, lambda r: wave_copy(n, r).wait_send())
        own_wave(n).wait()


def exchange(grid):
    n_gx, n_gy = lax.axis_size("gx"), lax.axis_size("gy")
    devices = n_gx * n_gy
    cells_y, cells_x, _ = grid.shape
    tall = cells_y // n_gx
    chunks_y = tall // 8 if tall % 8 == 0 else 1
    padded = -(-tall // 8) * 8
    modes = KX // devices
    phase_x = phases(KX, NX, NX)
    scale = 1.0 / math.sqrt(NX * NY)
    table = np.concatenate([np.cos(phase_x) * scale, -np.sin(phase_x) * scale], 0)
    high = table.astype(jnp.bfloat16)
    low = (table - high.astype(np.float64)).astype(jnp.bfloat16)
    count = 2 * chunks_y
    dma = pltpu.SemaphoreType.DMA
    vmem = pl.BlockSpec(memory_space=pltpu.VMEM)
    out = pl.pallas_call(
        functools.partial(exchange_kernel, n_gx, n_gy, chunks_y),
        out_shape=jax.ShapeDtypeStruct((2, modes, devices, padded, NZ), jnp.float32),
        in_specs=[pl.BlockSpec(memory_space=pl.ANY), vmem, vmem],
        out_specs=pl.BlockSpec(memory_space=pl.ANY),
        scratch_shapes=[
            pltpu.VMEM((tall, NX, NZ), jnp.float32),
            pltpu.VMEM((2, KX, padded, NZ), jnp.float32),
            dma((count, n_gx)),
            dma((count, n_gx)),
            dma((count, devices)),
            dma((count, devices)),
            dma((count,)),
            dma((count,)),
        ],
        compiler_params=pltpu.CompilerParams(
            collective_id=0, has_side_effects=True, vmem_limit_bytes=48 * 1024 * 1024
        ),
    )(grid, jnp.asarray(high), jnp.asarray(low))
    return out[:, :, :, :tall].reshape(2, modes, NY, NZ)


def per_device(multipoles, fractions, base_index, block_plane, atom_count, coupling):
    cells_x = NX // lax.axis_size("gx")
    cells_y = NY // lax.axis_size("gy")
    extended = spread(
        multipoles, fractions, base_index, block_plane, atom_count, cells_x, cells_y
    )
    rim_x = from_behind(extended[cells_x:, : cells_y + 3], "gx", 1)
    spill = extended[:cells_x, cells_y : cells_y + 3].at[:3].add(rim_x[:, cells_y:])
    rim_y = from_behind(spill, "gy", 1)
    density = (
        extended[:cells_x, :cells_y]
        + jnp.pad(rim_x[:, :cells_y], ((0, cells_x - 3), (0, 0), (0, 0)))
        + jnp.pad(rim_y, ((0, 0), (0, cells_y - 3), (0, 0)))
    )
    spectrum = exchange(density.transpose(1, 0, 2))
    phase_y = phases(NY, NY, NY)
    cosine, sine = np.cos(phase_y), np.sin(phase_y)
    table_y = jnp.asarray(np.stack([np.stack([cosine, sine]), np.stack([-sine, cosine])]), jnp.float32)
    waves = jnp.einsum("cdqr,dkrz->ckqz", table_y, spectrum, precision=lax.Precision.HIGH)
    mode_rows = waves.shape[1]
    stacked = waves.reshape(2, mode_rows, MBLK, NY // MBLK, NZ)
    coupled = jnp.einsum("ckbjw,bzw->ckbjz", stacked, coupling)
    return coupled.reshape(2, mode_rows, NY, NZ)


def solution(mesh):
    return jax.shard_map(
        per_device,
        mesh=mesh,
        in_specs=(
            P(None, ("gx", "gy")),
            P(None, ("gx", "gy")),
            P(None, ("gx", "gy")),
            P(("gx", "gy")),
            P(("gx", "gy")),
            P(),
        ),
        out_specs=P(None, ("gx", "gy"), None, None),
        check_vma=False,
    )
```

```python
import functools
import math

import jax
import jax.numpy as jnp
import numpy as np
from jax import lax
from jax.experimental import pallas as pl
from jax.experimental.pallas import tpu as pltpu
from jax.sharding import PartitionSpec as P

NX = 512
NY = 512
NZ = 256
XB = 8
SLOT_BLK = 128
MBLK = 8
KX = 256
GROUP = 8
PACK = 16


def from_behind(value, axis, by):
    devices = lax.axis_size(axis)
    return lax.ppermute(value, axis, [(i, (i + by) % devices) for i in range(devices)])


def spline_weights(u):
    r = 1.0 - u
    square = u * u
    cubed = square * u
    values = [
        r * r * r / 6.0,
        (3.0 * cubed - 6.0 * square + 4.0) / 6.0,
        (-3.0 * cubed + 3.0 * square + 3.0 * u + 1.0) / 6.0,
        cubed / 6.0,
    ]
    slopes = [
        -r * r / 2.0,
        (3.0 * square - 4.0 * u) / 2.0,
        (-3.0 * square + 2.0 * u + 1.0) / 2.0,
        square / 2.0,
    ]
    curves = [r, 3.0 * u - 2.0, 1.0 - 3.0 * u, u]
    return values, slopes, curves


def spread_kernel(
    plane_ref, count_ref, moment_ref, fraction_ref, cell_ref, out_ref, weight_ref, rows_ref
):
    step = pl.program_id(0)
    rows = out_ref.shape[1]
    padded = rows_ref.shape[1]
    bf16 = jnp.bfloat16

    @pl.when(step == 0)
    def _():
        def clear(plane, carry):
            out_ref[plane] = jnp.zeros((rows, NZ), jnp.float32)
            return carry

        lax.fori_loop(0, out_ref.shape[0], clear, 0)

    wx, dx, sx = spline_weights(fraction_ref[0])
    wy, dy, sy = spline_weights(fraction_ref[1])
    z_taps = spline_weights(fraction_ref[2])
    m = [moment_ref[i] for i in range(10)]
    for a in range(4):
        base = m[0] * wx[a] + m[1] * dx[a] + m[4] * sx[a]
        slope = m[2] * wx[a] + m[7] * dx[a]
        curve = m[5] * wx[a]
        one_base = m[3] * wx[a] + m[8] * dx[a]
        one_slope = m[9] * wx[a]
        two = m[6] * wx[a]
        for b in range(4):
            weight_ref[a * 4 + b] = base * wy[b] + slope * dy[b] + curve * sy[b]
            weight_ref[16 + a * 4 + b] = one_base * wy[b] + one_slope * dy[b]
            weight_ref[32 + a * 4 + b] = two * wy[b]
    for k in range(3):
        for c in range(4):
            weight_ref[48 + k * 4 + c] = z_taps[k][c]

    lane = lax.broadcasted_iota(jnp.int32, (1, SLOT_BLK), 1)

    def spans(tile, count):
        return jnp.concatenate([tile] * count, axis=0)

    def packed(row):
        return jnp.broadcast_to(row, (PACK, SLOT_BLK)).astype(bf16)

    y_count = padded // PACK
    z_count = NZ // PACK

    def one_block(g, carry):
        block = step * GROUP + g
        alive = lane < count_ref[block]
        x_cell = packed(cell_ref[0, pl.ds(g, 1), :].astype(jnp.float32))
        y_row = jnp.where(alive, cell_ref[1, pl.ds(g, 1), :], -1024).astype(jnp.float32)
        z_row = cell_ref[2, pl.ds(g, 1), :].astype(jnp.float32)

        def weight(index):
            return packed(weight_ref[index, pl.ds(g, 1), :])

        def chosen(hits, index, count):
            zero = jnp.zeros((count * PACK, SLOT_BLK), bf16)
            total = zero
            for tap in range(4):
                total = jnp.where(hits[tap], spans(weight(index + tap), count), total)
            return total

        y_ids = lax.broadcasted_iota(jnp.int32, (padded, SLOT_BLK), 0).astype(jnp.float32)
        y_ids = y_ids.astype(bf16)
        y_hits = [y_ids == spans(packed(y_row + float(b)), y_count) for b in range(4)]
        for k in range(3):
            for a in range(4):
                rows_ref[k * 4 + a] = chosen(y_hits, k * 16 + a * 4, y_count)
        z_ids = lax.broadcasted_iota(jnp.int32, (NZ, SLOT_BLK), 0).astype(jnp.float32)
        z_ids = z_ids.astype(bf16)
        z_hits = [z_ids == spans(packed(z_row + float(c)), z_count) for c in range(4)]
        z_window = jnp.concatenate(
            [chosen(z_hits, 48 + k * 4, z_count) for k in range(3)], axis=1
        )
        plane = plane_ref[block] * XB
        zero = jnp.zeros((padded, SLOT_BLK), bf16)
        for first, count in ((0, 4), (4, 4), (8, 3)):
            parts = []
            for x in range(first, first + count):
                pieces = []
                for k in range(3):
                    total = zero
                    for a in range(4):
                        if 0 <= x - a < XB:
                            hit = x_cell == jnp.full((PACK, SLOT_BLK), x - a, bf16)
                            total = jnp.where(spans(hit, y_count), rows_ref[k * 4 + a], total)
                    pieces.append(total)
                parts.append(jnp.concatenate(pieces, axis=1))
            window = jnp.concatenate(parts, axis=0)
            result = lax.dot_general(
                window, z_window, (((1,), (1,)), ((), ())), preferred_element_type=jnp.float32
            )
            for i in range(count):
                out_ref[plane + first + i] += result[i * padded : i * padded + rows]
        return carry

    lax.fori_loop(0, GROUP, one_block, 0)


def spread(multipoles, fractions, base_index, block_plane, atom_count, cells_x, cells_y):
    blocks = block_plane.shape[0]
    rows = -(-(cells_y + 3) // 8) * 8
    padded = -(-(cells_y + 3) // PACK) * PACK

    def part(height):
        return pl.BlockSpec((height, GROUP, SLOT_BLK), lambda i, *_: (0, i, 0))

    return pl.pallas_call(
        spread_kernel,
        out_shape=jax.ShapeDtypeStruct((cells_x + 3, rows, NZ), jnp.float32),
        grid_spec=pltpu.PrefetchScalarGridSpec(
            num_scalar_prefetch=2,
            grid=(blocks // GROUP,),
            in_specs=[part(10), part(3), part(3)],
            out_specs=pl.BlockSpec((cells_x + 3, rows, NZ), lambda i, *_: (0, 0, 0)),
            scratch_shapes=[
                pltpu.VMEM((60, GROUP, SLOT_BLK), jnp.float32),
                pltpu.VMEM((12, padded, SLOT_BLK), jnp.bfloat16),
            ],
        ),
        compiler_params=pltpu.CompilerParams(vmem_limit_bytes=48 * 1024 * 1024),
    )(
        block_plane,
        atom_count,
        multipoles.reshape(10, blocks, SLOT_BLK),
        fractions.reshape(3, blocks, SLOT_BLK),
        base_index.reshape(3, blocks, SLOT_BLK),
    )


def phases(waves, cells, size):
    return (np.arange(waves)[:, None] * np.arange(cells)[None, :] % size) * (2.0 * math.pi / size)


def exchange_kernel(
    n_gx,
    n_gy,
    chunks_y,
    grid_ref,
    high_ref,
    low_ref,
    out_ref,
    lines_ref,
    waves_ref,
    send_x,
    recv_x,
    send_k,
    recv_k,
    own_x,
    own_k,
):
    gx = lax.axis_index("gx")
    gy = lax.axis_index("gy")
    devices = n_gx * n_gy
    tall, cells_x = lines_ref.shape[0], grid_ref.shape[1]
    height = tall // chunks_y
    padded = waves_ref.shape[2]
    tile = padded // chunks_y
    modes = KX // devices
    chunks = [(i, j) for j in range(2) for i in range(chunks_y)]
    f32, bf16 = jnp.float32, jnp.bfloat16

    def coords(r):
        return lax.rem(gx + r // n_gy, n_gx), lax.rem(gy + lax.rem(r, n_gy), n_gy)

    barrier = pltpu.get_barrier_semaphore()

    def greet(r, carry):
        tx, ty = coords(r)
        pl.semaphore_signal(
            barrier, inc=1, device_id=(tx, ty), device_id_type=pl.DeviceIdType.MESH
        )
        return carry

    lax.fori_loop(1, devices, greet, 0)
    pl.semaphore_wait(barrier, devices - 1)

    def line_refs(n, tx):
        i, j = chunks[n]
        lanes = pl.ds(j * 128, 128)
        source = grid_ref.at[pl.ds(tx * tall + i * height, height), :, lanes]
        target = lines_ref.at[
            pl.ds(i * height, height), pl.ds(pl.multiple_of(gx * cells_x, cells_x), cells_x), lanes
        ]
        return source, target

    def line_copy(n, r):
        tx = lax.rem(gx + r, n_gx)
        source, target = line_refs(n, tx)
        return pltpu.make_async_remote_copy(
            src_ref=source,
            dst_ref=target,
            send_sem=send_x.at[n, r],
            recv_sem=recv_x.at[n, r],
            device_id=(tx, gy),
            device_id_type=pl.DeviceIdType.MESH,
        )

    def wave_refs(n, rank):
        i, j = chunks[n]
        lanes = pl.ds(j * 128, 128)
        span = pl.ds(i * tile, tile)
        source = waves_ref.at[:, pl.ds(rank * modes, modes), span, lanes]
        target = out_ref.at[:, :, gy * n_gx + gx, span, lanes]
        return source, target

    def wave_copy(n, r):
        tx, ty = coords(r)
        source, target = wave_refs(n, tx * n_gy + ty)
        return pltpu.make_async_remote_copy(
            src_ref=source,
            dst_ref=target,
            send_sem=send_k.at[n, r],
            recv_sem=recv_k.at[n, r],
            device_id=(tx, ty),
            device_id_type=pl.DeviceIdType.MESH,
        )

    def own_line(n):
        source, target = line_refs(n, gx)
        return pltpu.make_async_copy(source, target, own_x.at[n])

    def own_wave(n):
        source, target = wave_refs(n, gx * n_gy + gy)
        return pltpu.make_async_copy(source, target, own_k.at[n])

    def each(first, last, act):
        def body(r, carry):
            act(r)
            return carry

        lax.fori_loop(first, last, body, 0)

    for n in range(len(chunks)):
        each(1, n_gx, lambda r: line_copy(n, r).start())
        own_line(n).start()
    for n, (i, j) in enumerate(chunks):
        each(1, n_gx, lambda r: line_copy(n, r).wait_recv())
        own_line(n).wait()
        lanes = pl.ds(j * 128, 128)
        for first in range(i * height, (i + 1) * height, 2):
            picked = [y for y in (first, first + 1) if y < (i + 1) * height]
            block = jnp.concatenate([lines_ref[y, :, lanes] for y in picked], axis=1)
            top = block.astype(bf16)
            rest = (block - top.astype(f32)).astype(bf16)
            high = high_ref[...]
            value = jnp.dot(high, top, preferred_element_type=f32)
            value += jnp.dot(high, rest, preferred_element_type=f32)
            value += jnp.dot(low_ref[...], top, preferred_element_type=f32)
            for index, y in enumerate(picked):
                row = y if tall % 8 == 0 else y - i * height
                part = value[:, index * 128 : (index + 1) * 128]
                waves_ref[0, :, row, lanes] = part[:KX]
                waves_ref[1, :, row, lanes] = part[KX:]
        each(1, devices, lambda r: wave_copy(n, r).start())
        own_wave(n).start()
    for n in range(len(chunks)):
        each(1, n_gx, lambda r: line_copy(n, r).wait_send())
        each(1, devices, lambda r: wave_copy(n, r).wait_recv())
        each(1, devices, lambda r: wave_copy(n, r).wait_send())
        own_wave(n).wait()


def exchange(grid):
    n_gx, n_gy = lax.axis_size("gx"), lax.axis_size("gy")
    devices = n_gx * n_gy
    cells_y, cells_x, _ = grid.shape
    tall = cells_y // n_gx
    chunks_y = tall // 8 if tall % 8 == 0 else 1
    padded = -(-tall // 8) * 8
    modes = KX // devices
    phase_x = phases(KX, NX, NX)
    scale = 1.0 / math.sqrt(NX * NY)
    table = np.concatenate([np.cos(phase_x) * scale, -np.sin(phase_x) * scale], 0)
    high = table.astype(jnp.bfloat16)
    low = (table - high.astype(np.float64)).astype(jnp.bfloat16)
    count = 2 * chunks_y
    dma = pltpu.SemaphoreType.DMA
    vmem = pl.BlockSpec(memory_space=pltpu.VMEM)
    out = pl.pallas_call(
        functools.partial(exchange_kernel, n_gx, n_gy, chunks_y),
        out_shape=jax.ShapeDtypeStruct((2, modes, devices, padded, NZ), jnp.float32),
        in_specs=[pl.BlockSpec(memory_space=pl.ANY), vmem, vmem],
        out_specs=pl.BlockSpec(memory_space=pl.ANY),
        scratch_shapes=[
            pltpu.VMEM((tall, NX, NZ), jnp.float32),
            pltpu.VMEM((2, KX, padded, NZ), jnp.float32),
            dma((count, n_gx)),
            dma((count, n_gx)),
            dma((count, devices)),
            dma((count, devices)),
            dma((count,)),
            dma((count,)),
        ],
        compiler_params=pltpu.CompilerParams(
            collective_id=0, has_side_effects=True, vmem_limit_bytes=48 * 1024 * 1024
        ),
    )(grid, jnp.asarray(high), jnp.asarray(low))
    return out[:, :, :, :tall].reshape(2, modes, NY, NZ)


def finish_kernel(table_ref, wave_ref, coupling_ref, out_ref):
    f32, bf16 = jnp.float32, jnp.bfloat16
    count = wave_ref.shape[1]
    rows = NY // MBLK
    data = [
        jnp.concatenate([wave_ref[0, i], wave_ref[1, i]], axis=0).astype(bf16)
        for i in range(count)
    ]
    data = jnp.concatenate(data, axis=1)

    def one_block(b, carry):
        start = pl.multiple_of(b * rows, rows)
        parts = []
        for c in range(2):
            table = table_ref[c, pl.ds(start, rows), :]
            value = jnp.dot(table, data, preferred_element_type=f32)
            parts += [value[:, i * NZ : (i + 1) * NZ] for i in range(count)]
        value = jnp.concatenate(parts, axis=0)
        matrix = coupling_ref[b]
        value_high = value.astype(bf16)
        value_low = (value - value_high.astype(f32)).astype(bf16)
        matrix_high = matrix.astype(bf16)
        matrix_low = (matrix - matrix_high.astype(f32)).astype(bf16)

        def mix(left, right):
            return lax.dot_general(
                left, right, (((1,), (1,)), ((), ())), preferred_element_type=f32
            )

        result = (
            mix(value_high, matrix_high)
            + mix(value_low, matrix_high)
            + mix(value_high, matrix_low)
        )
        for c in range(2):
            for i in range(count):
                first = (c * count + i) * rows
                out_ref[c, i, pl.ds(start, rows), :] = result[first : first + rows]
        return carry

    for b in range(MBLK):
        one_block(b, 0)


def finish(spectrum, coupling):
    modes = spectrum.shape[1]
    count = 2 if modes % 2 == 0 else 1
    phase_y = phases(NY, NY, NY)
    cosine, sine = np.cos(phase_y), np.sin(phase_y)
    table = np.stack(
        [np.concatenate([cosine, sine], 1), np.concatenate([-sine, cosine], 1)]
    ).astype(jnp.bfloat16)
    block = pl.BlockSpec((2, count, NY, NZ), lambda i: (0, i, 0, 0))
    return pl.pallas_call(
        finish_kernel,
        out_shape=jax.ShapeDtypeStruct((2, modes, NY, NZ), jnp.float32),
        grid=(modes // count,),
        in_specs=[
            pl.BlockSpec((2, NY, 2 * NY), lambda i: (0, 0, 0)),
            block,
            pl.BlockSpec((MBLK, NZ, NZ), lambda i: (0, 0, 0)),
        ],
        out_specs=block,
        compiler_params=pltpu.CompilerParams(vmem_limit_bytes=40 * 1024 * 1024),
    )(jnp.asarray(table), spectrum, coupling)


def per_device(multipoles, fractions, base_index, block_plane, atom_count, coupling):
    cells_x = NX // lax.axis_size("gx")
    cells_y = NY // lax.axis_size("gy")
    extended = spread(
        multipoles, fractions, base_index, block_plane, atom_count, cells_x, cells_y
    )
    rim_x = from_behind(extended[cells_x:, : cells_y + 3], "gx", 1)
    spill = extended[:cells_x, cells_y : cells_y + 3].at[:3].add(rim_x[:, cells_y:])
    rim_y = from_behind(spill, "gy", 1)
    density = (
        extended[:cells_x, :cells_y]
        + jnp.pad(rim_x[:, :cells_y], ((0, cells_x - 3), (0, 0), (0, 0)))
        + jnp.pad(rim_y, ((0, 0), (0, cells_y - 3), (0, 0)))
    )
    spectrum = exchange(density.transpose(1, 0, 2))
    return finish(spectrum, coupling)


def solution(mesh):
    return jax.shard_map(
        per_device,
        mesh=mesh,
        in_specs=(
            P(None, ("gx", "gy")),
            P(None, ("gx", "gy")),
            P(None, ("gx", "gy")),
            P(("gx", "gy")),
            P(("gx", "gy")),
            P(),
        ),
        out_specs=P(None, ("gx", "gy"), None, None),
        check_vma=False,
    )
```

```python
import functools
import math

import jax
import jax.numpy as jnp
import numpy as np
from jax import lax
from jax.experimental import pallas as pl
from jax.experimental.pallas import tpu as pltpu
from jax.sharding import PartitionSpec as P

NX = 512
NY = 512
NZ = 256
XB = 8
SLOT_BLK = 128
MBLK = 8
KX = 256
GROUP = 8
PACK = 16


def from_behind(value, axis, by):
    devices = lax.axis_size(axis)
    return lax.ppermute(value, axis, [(i, (i + by) % devices) for i in range(devices)])


def spline_weights(u):
    r = 1.0 - u
    square = u * u
    cubed = square * u
    values = [
        r * r * r / 6.0,
        (3.0 * cubed - 6.0 * square + 4.0) / 6.0,
        (-3.0 * cubed + 3.0 * square + 3.0 * u + 1.0) / 6.0,
        cubed / 6.0,
    ]
    slopes = [
        -r * r / 2.0,
        (3.0 * square - 4.0 * u) / 2.0,
        (-3.0 * square + 2.0 * u + 1.0) / 2.0,
        square / 2.0,
    ]
    curves = [r, 3.0 * u - 2.0, 1.0 - 3.0 * u, u]
    return values, slopes, curves


def spread_kernel(
    plane_ref, count_ref, moment_ref, fraction_ref, cell_ref, out_ref, weight_ref, rows_ref
):
    step = pl.program_id(0)
    rows = out_ref.shape[1]
    padded = rows_ref.shape[1]
    bf16 = jnp.bfloat16

    @pl.when(step == 0)
    def _():
        def clear(plane, carry):
            out_ref[plane] = jnp.zeros((rows, NZ), jnp.float32)
            return carry

        lax.fori_loop(0, out_ref.shape[0], clear, 0)

    wx, dx, sx = spline_weights(fraction_ref[0])
    wy, dy, sy = spline_weights(fraction_ref[1])
    z_taps = spline_weights(fraction_ref[2])
    m = [moment_ref[i] for i in range(10)]
    for a in range(4):
        base = m[0] * wx[a] + m[1] * dx[a] + m[4] * sx[a]
        slope = m[2] * wx[a] + m[7] * dx[a]
        curve = m[5] * wx[a]
        one_base = m[3] * wx[a] + m[8] * dx[a]
        one_slope = m[9] * wx[a]
        two = m[6] * wx[a]
        for b in range(4):
            weight_ref[a * 4 + b] = base * wy[b] + slope * dy[b] + curve * sy[b]
            weight_ref[16 + a * 4 + b] = one_base * wy[b] + one_slope * dy[b]
            weight_ref[32 + a * 4 + b] = two * wy[b]
    for k in range(3):
        for c in range(4):
            weight_ref[48 + k * 4 + c] = z_taps[k][c]

    lane = lax.broadcasted_iota(jnp.int32, (1, SLOT_BLK), 1)

    def spans(tile, count):
        return jnp.concatenate([tile] * count, axis=0)

    def packed(row):
        return jnp.broadcast_to(row, (PACK, SLOT_BLK)).astype(bf16)

    y_count = padded // PACK
    z_count = NZ // PACK

    def one_block(g, carry):
        block = step * GROUP + g
        alive = lane < count_ref[block]
        x_cell = packed(cell_ref[0, pl.ds(g, 1), :].astype(jnp.float32))
        y_row = jnp.where(alive, cell_ref[1, pl.ds(g, 1), :], -1024).astype(jnp.float32)
        z_row = cell_ref[2, pl.ds(g, 1), :].astype(jnp.float32)

        def weight(index):
            return packed(weight_ref[index, pl.ds(g, 1), :])

        def chosen(hits, index, count):
            zero = jnp.zeros((count * PACK, SLOT_BLK), bf16)
            total = zero
            for tap in range(4):
                total = jnp.where(hits[tap], spans(weight(index + tap), count), total)
            return total

        y_ids = lax.broadcasted_iota(jnp.int32, (padded, SLOT_BLK), 0).astype(jnp.float32)
        y_ids = y_ids.astype(bf16)
        y_hits = [y_ids == spans(packed(y_row + float(b)), y_count) for b in range(4)]
        for k in range(3):
            for a in range(4):
                rows_ref[k * 4 + a] = chosen(y_hits, k * 16 + a * 4, y_count)
        z_ids = lax.broadcasted_iota(jnp.int32, (NZ, SLOT_BLK), 0).astype(jnp.float32)
        z_ids = z_ids.astype(bf16)
        z_hits = [z_ids == spans(packed(z_row + float(c)), z_count) for c in range(4)]
        z_window = jnp.concatenate(
            [chosen(z_hits, 48 + k * 4, z_count) for k in range(3)], axis=1
        )
        plane = plane_ref[block] * XB
        zero = jnp.zeros((padded, SLOT_BLK), bf16)
        for first, count in ((0, 4), (4, 4), (8, 3)):
            parts = []
            for x in range(first, first + count):
                pieces = []
                for k in range(3):
                    total = zero
                    for a in range(4):
                        if 0 <= x - a < XB:
                            hit = x_cell == jnp.full((PACK, SLOT_BLK), x - a, bf16)
                            total = jnp.where(spans(hit, y_count), rows_ref[k * 4 + a], total)
                    pieces.append(total)
                parts.append(jnp.concatenate(pieces, axis=1))
            window = jnp.concatenate(parts, axis=0)
            result = lax.dot_general(
                window, z_window, (((1,), (1,)), ((), ())), preferred_element_type=jnp.float32
            )
            for i in range(count):
                out_ref[plane + first + i] += result[i * padded : i * padded + rows]
        return carry

    lax.fori_loop(0, GROUP, one_block, 0)


def spread(multipoles, fractions, base_index, block_plane, atom_count, cells_x, cells_y):
    blocks = block_plane.shape[0]
    rows = -(-(cells_y + 3) // 8) * 8
    padded = -(-(cells_y + 3) // PACK) * PACK

    def part(height):
        return pl.BlockSpec((height, GROUP, SLOT_BLK), lambda i, *_: (0, i, 0))

    return pl.pallas_call(
        spread_kernel,
        out_shape=jax.ShapeDtypeStruct((cells_x + 3, rows, NZ), jnp.float32),
        grid_spec=pltpu.PrefetchScalarGridSpec(
            num_scalar_prefetch=2,
            grid=(blocks // GROUP,),
            in_specs=[part(10), part(3), part(3)],
            out_specs=pl.BlockSpec((cells_x + 3, rows, NZ), lambda i, *_: (0, 0, 0)),
            scratch_shapes=[
                pltpu.VMEM((60, GROUP, SLOT_BLK), jnp.float32),
                pltpu.VMEM((12, padded, SLOT_BLK), jnp.bfloat16),
            ],
        ),
        compiler_params=pltpu.CompilerParams(vmem_limit_bytes=48 * 1024 * 1024),
    )(
        block_plane,
        atom_count,
        multipoles.reshape(10, blocks, SLOT_BLK),
        fractions.reshape(3, blocks, SLOT_BLK),
        base_index.reshape(3, blocks, SLOT_BLK),
    )


def phases(waves, cells, size):
    return (np.arange(waves)[:, None] * np.arange(cells)[None, :] % size) * (2.0 * math.pi / size)


def exchange_kernel(
    n_gx,
    n_gy,
    chunks_y,
    grid_ref,
    high_ref,
    low_ref,
    out_ref,
    lines_ref,
    waves_ref,
    send_x,
    recv_x,
    send_k,
    recv_k,
    own_x,
    own_k,
):
    gx = lax.axis_index("gx")
    gy = lax.axis_index("gy")
    devices = n_gx * n_gy
    tall, cells_x = lines_ref.shape[0], grid_ref.shape[1]
    height = tall // chunks_y
    padded = waves_ref.shape[2]
    tile = padded // chunks_y
    modes = KX // devices
    chunks = [(i, j) for j in range(2) for i in range(chunks_y)]
    f32, bf16 = jnp.float32, jnp.bfloat16

    def coords(r):
        return lax.rem(gx + r // n_gy, n_gx), lax.rem(gy + lax.rem(r, n_gy), n_gy)

    barrier = pltpu.get_barrier_semaphore()

    def greet(r, carry):
        tx, ty = coords(r)
        pl.semaphore_signal(
            barrier, inc=1, device_id=(tx, ty), device_id_type=pl.DeviceIdType.MESH
        )
        return carry

    lax.fori_loop(1, devices, greet, 0)
    pl.semaphore_wait(barrier, devices - 1)

    def line_refs(n, tx):
        i, j = chunks[n]
        lanes = pl.ds(j * 128, 128)
        source = grid_ref.at[pl.ds(tx * tall + i * height, height), :, lanes]
        target = lines_ref.at[
            pl.ds(i * height, height), pl.ds(pl.multiple_of(gx * cells_x, cells_x), cells_x), lanes
        ]
        return source, target

    def line_copy(n, r):
        tx = lax.rem(gx + r, n_gx)
        source, target = line_refs(n, tx)
        return pltpu.make_async_remote_copy(
            src_ref=source,
            dst_ref=target,
            send_sem=send_x.at[n, r],
            recv_sem=recv_x.at[n, r],
            device_id=(tx, gy),
            device_id_type=pl.DeviceIdType.MESH,
        )

    def wave_refs(n, rank):
        i, j = chunks[n]
        lanes = pl.ds(j * 128, 128)
        span = pl.ds(i * tile, tile)
        source = waves_ref.at[:, pl.ds(rank * modes, modes), span, lanes]
        target = out_ref.at[:, :, gy * n_gx + gx, span, lanes]
        return source, target

    def wave_copy(n, r):
        tx, ty = coords(r)
        source, target = wave_refs(n, tx * n_gy + ty)
        return pltpu.make_async_remote_copy(
            src_ref=source,
            dst_ref=target,
            send_sem=send_k.at[n, r],
            recv_sem=recv_k.at[n, r],
            device_id=(tx, ty),
            device_id_type=pl.DeviceIdType.MESH,
        )

    def own_line(n):
        source, target = line_refs(n, gx)
        return pltpu.make_async_copy(source, target, own_x.at[n])

    def own_wave(n):
        source, target = wave_refs(n, gx * n_gy + gy)
        return pltpu.make_async_copy(source, target, own_k.at[n])

    def each(first, last, act):
        def body(r, carry):
            act(r)
            return carry

        lax.fori_loop(first, last, body, 0)

    for n in range(len(chunks)):
        each(1, n_gx, lambda r: line_copy(n, r).start())
        own_line(n).start()
    for n, (i, j) in enumerate(chunks):
        each(1, n_gx, lambda r: line_copy(n, r).wait_recv())
        own_line(n).wait()
        lanes = pl.ds(j * 128, 128)
        columns = []
        for first in range(i * height, (i + 1) * height, 2):
            picked = [y for y in (first, first + 1) if y < (i + 1) * height]
            block = jnp.concatenate([lines_ref[y, :, lanes] for y in picked], axis=1)
            top = block.astype(bf16)
            rest = (block - top.astype(f32)).astype(bf16)
            high = high_ref[...]
            value = jnp.dot(high, top, preferred_element_type=f32)
            value += jnp.dot(high, rest, preferred_element_type=f32)
            value += jnp.dot(low_ref[...], top, preferred_element_type=f32)
            columns += [value[:, m * 128 : (m + 1) * 128] for m in range(len(picked))]
        columns += [jnp.zeros_like(columns[0])] * (tile - height)
        turned = jnp.swapaxes(jnp.stack(columns, axis=0), 0, 1)
        waves_ref[0, :, i * tile : (i + 1) * tile, lanes] = turned[:KX]
        waves_ref[1, :, i * tile : (i + 1) * tile, lanes] = turned[KX:]
        each(1, devices, lambda r: wave_copy(n, r).start())
        own_wave(n).start()
    for n in range(len(chunks)):
        each(1, n_gx, lambda r: line_copy(n, r).wait_send())
        each(1, devices, lambda r: wave_copy(n, r).wait_recv())
        each(1, devices, lambda r: wave_copy(n, r).wait_send())
        own_wave(n).wait()


def exchange(grid):
    n_gx, n_gy = lax.axis_size("gx"), lax.axis_size("gy")
    devices = n_gx * n_gy
    cells_y, cells_x, _ = grid.shape
    tall = cells_y // n_gx
    chunks_y = tall // 8 if tall % 8 == 0 else 1
    padded = -(-tall // 8) * 8
    modes = KX // devices
    phase_x = phases(KX, NX, NX)
    scale = 1.0 / math.sqrt(NX * NY)
    table = np.concatenate([np.cos(phase_x) * scale, -np.sin(phase_x) * scale], 0)
    high = table.astype(jnp.bfloat16)
    low = (table - high.astype(np.float64)).astype(jnp.bfloat16)
    count = 2 * chunks_y
    dma = pltpu.SemaphoreType.DMA
    vmem = pl.BlockSpec(memory_space=pltpu.VMEM)
    out = pl.pallas_call(
        functools.partial(exchange_kernel, n_gx, n_gy, chunks_y),
        out_shape=jax.ShapeDtypeStruct((2, modes, devices, padded, NZ), jnp.float32),
        in_specs=[pl.BlockSpec(memory_space=pl.ANY), vmem, vmem],
        out_specs=pl.BlockSpec(memory_space=pl.ANY),
        scratch_shapes=[
            pltpu.VMEM((tall, NX, NZ), jnp.float32),
            pltpu.VMEM((2, KX, padded, NZ), jnp.float32),
            dma((count, n_gx)),
            dma((count, n_gx)),
            dma((count, devices)),
            dma((count, devices)),
            dma((count,)),
            dma((count,)),
        ],
        compiler_params=pltpu.CompilerParams(
            collective_id=0, has_side_effects=True, vmem_limit_bytes=48 * 1024 * 1024
        ),
    )(grid, jnp.asarray(high), jnp.asarray(low))
    return out[:, :, :, :tall].reshape(2, modes, NY, NZ)


def finish_kernel(table_ref, wave_ref, coupling_ref, out_ref, rows_ref):
    f32, bf16 = jnp.float32, jnp.bfloat16
    count = wave_ref.shape[1]
    rows = NY // MBLK
    data = [
        jnp.concatenate([wave_ref[0, i], wave_ref[1, i]], axis=0).astype(bf16)
        for i in range(count)
    ]
    data = jnp.concatenate(data, axis=1)
    for c in range(2):
        rows_ref[c] = jnp.dot(table_ref[c], data, preferred_element_type=f32)

    def one_block(b, carry):
        start = b * rows
        parts = []
        for c in range(2):
            value = rows_ref[c, pl.ds(start, rows), :]
            parts += [value[:, i * NZ : (i + 1) * NZ] for i in range(count)]
        value = jnp.concatenate(parts, axis=0)
        matrix = coupling_ref[b]
        value_high = value.astype(bf16)
        value_low = (value - value_high.astype(f32)).astype(bf16)
        matrix_high = matrix.astype(bf16)
        matrix_low = (matrix - matrix_high.astype(f32)).astype(bf16)

        def mix(left, right):
            return lax.dot_general(
                left, right, (((1,), (1,)), ((), ())), preferred_element_type=f32
            )

        result = (
            mix(value_high, matrix_high)
            + mix(value_low, matrix_high)
            + mix(value_high, matrix_low)
        )
        for c in range(2):
            for i in range(count):
                first = (c * count + i) * rows
                out_ref[c, i, pl.ds(start, rows), :] = result[first : first + rows]
        return carry

    for b in range(MBLK):
        one_block(b, 0)


def finish(spectrum, coupling):
    modes = spectrum.shape[1]
    count = 2 if modes % 2 == 0 else 1
    phase_y = phases(NY, NY, NY)
    cosine, sine = np.cos(phase_y), np.sin(phase_y)
    table = np.stack(
        [np.concatenate([cosine, sine], 1), np.concatenate([-sine, cosine], 1)]
    ).astype(jnp.bfloat16)
    block = pl.BlockSpec((2, count, NY, NZ), lambda i: (0, i, 0, 0))
    return pl.pallas_call(
        finish_kernel,
        out_shape=jax.ShapeDtypeStruct((2, modes, NY, NZ), jnp.float32),
        grid=(modes // count,),
        in_specs=[
            pl.BlockSpec((2, NY, 2 * NY), lambda i: (0, 0, 0)),
            block,
            pl.BlockSpec((MBLK, NZ, NZ), lambda i: (0, 0, 0)),
        ],
        out_specs=block,
        scratch_shapes=[pltpu.VMEM((2, NY, count * NZ), jnp.float32)],
        compiler_params=pltpu.CompilerParams(vmem_limit_bytes=40 * 1024 * 1024),
    )(jnp.asarray(table), spectrum, coupling)


def per_device(multipoles, fractions, base_index, block_plane, atom_count, coupling):
    cells_x = NX // lax.axis_size("gx")
    cells_y = NY // lax.axis_size("gy")
    extended = spread(
        multipoles, fractions, base_index, block_plane, atom_count, cells_x, cells_y
    )
    rim_x = from_behind(extended[cells_x:, : cells_y + 3], "gx", 1)
    spill = extended[:cells_x, cells_y : cells_y + 3].at[:3].add(rim_x[:, cells_y:])
    rim_y = from_behind(spill, "gy", 1)
    density = (
        extended[:cells_x, :cells_y]
        + jnp.pad(rim_x[:, :cells_y], ((0, cells_x - 3), (0, 0), (0, 0)))
        + jnp.pad(rim_y, ((0, 0), (0, cells_y - 3), (0, 0)))
    )
    spectrum = exchange(density.transpose(1, 0, 2))
    return finish(spectrum, coupling)


def solution(mesh):
    return jax.shard_map(
        per_device,
        mesh=mesh,
        in_specs=(
            P(None, ("gx", "gy")),
            P(None, ("gx", "gy")),
            P(None, ("gx", "gy")),
            P(("gx", "gy")),
            P(("gx", "gy")),
            P(),
        ),
        out_specs=P(None, ("gx", "gy"), None, None),
        check_vma=False,
    )
```
